32 devices in a mesh: parts: 2 (over y), blk: 4 (over z), owner: 2 (over x), sub: 2 (over core).
Axes of the slice: x: 2, y: 2, z: 4, core: 2. Of those that a mesh axis runs over, the one named last changes fastest.
Arguments:
- embeddings: bfloat16 [4096, 512], P(('parts', 'blk', 'owner', 'sub')), parts along dimension 0
- clusters: int32 [4096], P(('parts', 'blk', 'owner', 'sub')), parts along dimension 0, may hold values from 0 to 7
- place: int32 [4096], P(('parts', 'blk', 'owner', 'sub')), parts along dimension 0, may hold values from 0 to 255, as said below
Outputs:
- max_sim: float32 [4096], P(('parts', 'blk', 'owner', 'sub')), parts along dimension 0
The draws below stay inside these ranges and needn't reach their ends.
There are 2 independent parts, one for each index of `parts`. The reference program is written for one: setup_inputs(seed, part) draws one part's arguments, and reference() takes and returns one part's arrays. A program takes and returns all parts, laid end to end along the dimension named above; each array names one. Nothing has to cross between parts.
Inputs may be any that keep to these rules, and one draw needn't show every extreme that they name: place // 32 is a device index along blk and owner together, blk slowest; the places of the rows of one device are distinct; in every draw some destination receives all 32 of its slots from every device of one sub index.
All inputs are finite; a program needn't handle non-finite values.
Results may differ from the reference program's by a relative error of at most 0.00065.
Values may be sent and summed in bfloat16 or wider, within the bound.
A program may use at most 64 MiB of HBM per device.

```python
import math
import jax
import jax.numpy as jnp
from jax import lax

E = 512
ROW_DEV = 128
CLU_GRP = 2
CAP = 32
ROWS = 2048
CLUSTERS = 8
N_BLK = 4
N_OWNER = 2
N_SUB = 2


def routing(key):
    dest_count = N_BLK * N_OWNER
    devices = dest_count * N_SUB
    positions_all = dest_count * CAP
    filled = jax.random.randint(jax.random.fold_in(key, 11), (N_SUB,), 0, dest_count)
    positions = jnp.arange(positions_all, dtype=jnp.int32)
    target = positions // CAP
    offset = positions % CAP

    def one_device(device):
        dev_key = jax.random.fold_in(jax.random.fold_in(key, 12), device)
        sub_index = device % N_SUB
        shuffled = jax.random.permutation(dev_key, positions_all).astype(jnp.int32)
        edges = (positions == 0) | (positions == positions_all - 1)
        classes = jnp.where(target == filled[sub_index], 0, jnp.where(edges, 1, jnp.where(offset == 0, 2, 3)))
        scores = classes * positions_all + shuffled
        chosen = jnp.argsort(scores)[:ROW_DEV].astype(jnp.int32)
        chosen = jax.random.permutation(jax.random.fold_in(dev_key, 1), chosen)
        cluster_key = jax.random.fold_in(dev_key, 2)
        upper = jax.random.randint(cluster_key, (ROW_DEV,), 1, CLU_GRP + 1)
        local = jax.random.randint(jax.random.fold_in(cluster_key, 1), (ROW_DEV,), 0, CLU_GRP) % upper
        local = jnp.where(chosen == positions_all - 1, CLU_GRP - 1, jnp.where(chosen == 0, 0, local))
        owner_index = chosen // CAP % N_OWNER
        cluster = (owner_index * N_SUB + sub_index) * CLU_GRP + local
        return (chosen, cluster.astype(jnp.int32))
    places, cluster_ids = jax.vmap(one_device)(jnp.arange(devices, dtype=jnp.int32))
    return (places.reshape(-1), cluster_ids.reshape(-1))


def draw_place(key, part):
    shared = routing(key)
    return shared[0].astype(jnp.int32)


def draw_clusters(key, part):
    shared = routing(key)
    return shared[1].astype(jnp.int32)


def draw_embeddings(key, part):
    cluster_ids = routing(key)[1]
    key = jax.random.fold_in(key, 3)
    centers = jax.random.normal(jax.random.fold_in(key, 1), (CLUSTERS, E), jnp.float32)
    noise = jax.random.normal(jax.random.fold_in(key, 2), (ROWS, E), jnp.float32)
    common = jax.random.normal(jax.random.fold_in(key, 6), (ROWS // 2, E), jnp.float32)
    column = jnp.exp(jax.random.uniform(jax.random.fold_in(key, 5), (1, E), jnp.float32, math.log(0.5), math.log(2.0)))
    level = jnp.exp(jax.random.uniform(jax.random.fold_in(key, 3), (ROWS, 1), jnp.float32, math.log(0.08), math.log(1.5)))
    row_scale = jnp.exp(jax.random.uniform(jax.random.fold_in(key, 4), (ROWS, 1), jnp.float32, math.log(0.3), math.log(3.0)))
    tiebreak = jax.random.permutation(jax.random.fold_in(key, 7), ROWS).astype(jnp.int32)
    order = jnp.argsort(cluster_ids * ROWS + tiebreak).astype(jnp.int32)
    rank = jnp.zeros((ROWS,), jnp.int32).at[order].set(jnp.arange(ROWS, dtype=jnp.int32))
    pair_id = rank // 2
    paired = jax.random.randint(jax.random.fold_in(key, 8), (ROWS // 2,), 0, 2)[pair_id] == 1
    mixed = jnp.where(paired[:, None], 1.5 * common[pair_id] + 0.1 * noise, level * noise)
    values = (centers[cluster_ids] + mixed) * row_scale * column
    return values.astype(jnp.bfloat16)


def setup_inputs(seed: int = 0, part: int = 0) -> dict:
    key_of = jax.random.split(jax.random.key(seed), 4)
    part_splits = jax.random.split(jax.random.fold_in(key_of[3], part), 4)
    return {
        "embeddings": draw_embeddings(jax.random.fold_in(jax.random.fold_in(key_of[3], part), 71), part),
        "clusters": draw_clusters(jax.random.fold_in(jax.random.fold_in(key_of[3], part), 71), part),
        "place": draw_place(jax.random.fold_in(jax.random.fold_in(key_of[3], part), 71), part),
    }


def reference(embeddings, clusters, place):
    values = embeddings.astype(jnp.float32)
    scaled = values * lax.rsqrt(lax.optimization_barrier(jnp.mean(values * values, axis=1, keepdims=True)) + 1e-06) / math.sqrt(E)
    rounded = lax.optimization_barrier(scaled.astype(jnp.bfloat16))
    unit_rows = rounded.astype(jnp.float32)
    total = place.shape[0]
    row_ids = jnp.arange(total, dtype=jnp.int32)
    sub_index = row_ids // ROW_DEV % N_SUB
    group = place // CAP % N_OWNER * N_SUB + sub_index
    match_key = group * CLUSTERS + clusters
    block = math.gcd(total, 1024)

    def one_block(start):
        mine = lax.dynamic_slice_in_dim(unit_rows, start, block, 0)
        mine_key = lax.dynamic_slice_in_dim(match_key, start, block, 0)
        scores = jnp.dot(mine, unit_rows.T, precision=lax.Precision.HIGHEST)
        own_ids = start + jnp.arange(block, dtype=jnp.int32)
        allowed = (mine_key[:, None] == match_key[None, :]) & (own_ids[:, None] != row_ids[None, :])
        return lax.optimization_barrier(jnp.max(jnp.where(allowed, scores, -1.0), axis=1))
    starts = jnp.arange(total // block, dtype=jnp.int32) * block
    return lax.map(one_block, starts).reshape(total)
```

```python
import functools
import math

import jax
import jax.numpy as jnp
from jax import lax
from jax.experimental import pallas as pl
from jax.experimental.pallas import tpu as pltpu
from jax.sharding import PartitionSpec as P

MESH = pl.DeviceIdType.MESH
LOWEST = -1.0


def each(start, stop, step):
    if stop - start <= 8:
        for index in range(start, stop):
            step(index)
    else:
        lax.fori_loop(start, stop, lambda index, _: (step(index), 0)[1], 0)


def pair_scores(mine, other):
    return lax.dot_general(
        mine, other, (((1,), (1,)), ((), ())), preferred_element_type=jnp.float32
    )


def div_rem(values, cap, n_own):
    return lax.rem(lax.div(values, jnp.int32(cap)), jnp.int32(n_own))


def kernel(
    n_blk, n_own, cap,
    emb_ref, clusters_ref, place_ref, out_ref,
    emb, rows, row_keys, cols, col_keys, best,
    col_answer, col_back, row_answer, row_back,
    load_sem, col_send, col_recv, row_send, row_recv,
    col_back_send, col_back_recv, row_back_send, row_back_recv,
):
    n_rows, width = emb.shape
    z = lax.axis_index("blk")
    x = lax.axis_index("owner")
    sub = lax.axis_index("sub")
    pos = jnp.where(sub == 0, z, n_blk - 1 - z)
    sign = 1 - 2 * sub

    load = pltpu.make_async_copy(emb_ref, emb, load_sem)
    load.start()

    barrier = pltpu.get_barrier_semaphore()
    each(1, n_own, lambda e: pl.semaphore_signal(
        barrier, inc=1, device_id={"owner": lax.rem(x + e, n_own)}, device_id_type=MESH))
    each(1, n_blk, lambda d: pl.semaphore_signal(
        barrier, inc=1, device_id={"blk": lax.rem(z + d, n_blk)}, device_id_type=MESH))

    def col_copies(d):
        target = {"blk": jnp.clip(z + sign * d, 0, n_blk - 1)}
        return [
            pltpu.make_async_remote_copy(
                src_ref=src, dst_ref=dst, send_sem=col_send.at[d, k], recv_sem=col_recv.at[d, k],
                device_id=target, device_id_type=MESH)
            for k, (src, dst) in enumerate((
                (row_keys.at[0], col_keys.at[d]), (rows.at[pl.ds(0, n_rows)], cols.at[d])))
        ]

    def row_copies(e):
        target = {"owner": lax.rem(x + e, n_own)}
        return [
            pltpu.make_async_remote_copy(
                src_ref=src, dst_ref=dst, send_sem=row_send.at[e, k], recv_sem=row_recv.at[e, k],
                device_id=target, device_id_type=MESH)
            for k, (src, dst) in enumerate((
                (row_keys.at[0], row_keys.at[e]),
                (rows.at[pl.ds(0, n_rows)], rows.at[pl.ds(e * n_rows, n_rows)])))
        ]

    def col_return(d):
        return pltpu.make_async_remote_copy(
            src_ref=col_answer.at[d], dst_ref=col_back.at[d],
            send_sem=col_back_send.at[d], recv_sem=col_back_recv.at[d],
            device_id={"blk": jnp.clip(z - sign * d, 0, n_blk - 1)}, device_id_type=MESH)

    def row_return(e):
        return pltpu.make_async_remote_copy(
            src_ref=row_answer.at[e], dst_ref=row_back.at[e],
            send_sem=row_back_send.at[e], recv_sem=row_back_recv.at[e],
            device_id={"owner": lax.rem(x + n_own - e, n_own)}, device_id_type=MESH)

    group = div_rem(place_ref[...], cap, n_own)
    my_key = group * 65536 + clusters_ref[...]
    row_keys[0] = my_key
    load.wait()
    values = emb[...].astype(jnp.float32)
    mean = jnp.mean(values * values, axis=1, keepdims=True)
    unit = values * (lax.rsqrt(mean + 1e-06) * (1.0 / math.sqrt(width)))
    rows[pl.ds(0, n_rows)] = unit.astype(jnp.bfloat16)

    pl.semaphore_wait(barrier, n_blk - 1 + n_own - 1)

    def send_cols(d):
        @pl.when(pos + d < n_blk)
        def _():
            for copy in col_copies(d):
                copy.start()

    each(1, n_blk, send_cols)

    def send_rows(e):
        for copy in row_copies(e):
            copy.start()

    each(1, n_own, send_rows)

    def down(key):
        return jnp.transpose(jnp.broadcast_to(key, (n_rows, n_rows)))

    my_down = down(my_key)
    mine = rows[pl.ds(0, n_rows)]
    shape = (n_rows, n_rows)
    other = lax.broadcasted_iota(jnp.int32, shape, 0) != lax.broadcasted_iota(jnp.int32, shape, 1)
    best[pl.ds(0, n_rows)] = jnp.where(
        (my_down == my_key) & other, pair_scores(mine, mine), LOWEST)

    def meet_row(e):
        for copy in row_copies(e):
            copy.wait_recv()
        theirs = rows[pl.ds(e * n_rows, n_rows)]
        found = jnp.where(my_down == row_keys[e], pair_scores(mine, theirs), LOWEST)
        best[pl.ds(0, n_rows)] = jnp.maximum(best[pl.ds(0, n_rows)], found)
        best[pl.ds(e * n_rows, n_rows)] = jnp.full(shape, LOWEST, jnp.float32)

    each(1, n_own, meet_row)

    def meet_col(d):
        @pl.when(pos >= d)
        def _():
            for copy in col_copies(d):
                copy.wait_recv()
            col_key = col_keys[d]
            scores = pair_scores(rows[...], cols[d])
            answer = None
            for e in range(n_own):
                here = pl.ds(e * n_rows, n_rows)
                found = jnp.where(
                    down(row_keys[e]) == col_key, scores[e * n_rows:(e + 1) * n_rows], LOWEST)
                best[here] = jnp.maximum(best[here], found)
                top = jnp.max(found, axis=0, keepdims=True)
                answer = top if answer is None else jnp.maximum(answer, top)
            col_answer[d] = answer
            col_return(d).start()

    each(1, n_blk, meet_col)

    def answer_row(e):
        @pl.when(pos > 0)
        def _():
            row_answer[e] = jnp.max(
                jnp.transpose(best[pl.ds(e * n_rows, n_rows)]), axis=0, keepdims=True)
            row_return(e).start()

    each(1, n_own, answer_row)

    out_ref[...] = jnp.max(jnp.transpose(best[pl.ds(0, n_rows)]), axis=0, keepdims=True)

    def take_row(e):
        for copy in row_copies(e):
            copy.wait_send()

        @pl.when(pos > 0)
        def _():
            row_return(e).wait()
            out_ref[...] = jnp.maximum(out_ref[...], row_back[e])

    def take_col(d):
        @pl.when(pos + d < n_blk)
        def _():
            for copy in col_copies(d):
                copy.wait_send()
            col_return(d).wait_recv()
            out_ref[...] = jnp.maximum(out_ref[...], col_back[d])

        @pl.when(pos >= d)
        def _():
            col_return(d).wait_send()

    each(1, n_own, take_row)
    each(1, n_blk, take_col)


def body(embeddings, clusters, place):
    n_rows, width = embeddings.shape
    n_blk = lax.axis_size("blk")
    n_own = lax.axis_size("owner")
    cap = 2 * n_rows // (n_blk * n_own)
    vmem = pl.BlockSpec(memory_space=pltpu.VMEM)
    dma = pltpu.SemaphoreType.DMA
    best = pl.pallas_call(
        functools.partial(kernel, n_blk, n_own, cap),
        out_shape=jax.ShapeDtypeStruct((1, n_rows), jnp.float32),
        in_specs=[pl.BlockSpec(memory_space=pl.ANY), vmem, vmem],
        out_specs=vmem,
        scratch_shapes=[
            pltpu.VMEM((n_rows, width), jnp.bfloat16),
            pltpu.VMEM((n_own * n_rows, width), jnp.bfloat16),
            pltpu.VMEM((n_own, 1, n_rows), jnp.int32),
            pltpu.VMEM((n_blk, n_rows, width), jnp.bfloat16),
            pltpu.VMEM((n_blk, 1, n_rows), jnp.int32),
            pltpu.VMEM((n_own * n_rows, n_rows), jnp.float32),
            pltpu.VMEM((n_blk, 1, n_rows), jnp.float32),
            pltpu.VMEM((n_blk, 1, n_rows), jnp.float32),
            pltpu.VMEM((n_own, 1, n_rows), jnp.float32),
            pltpu.VMEM((n_own, 1, n_rows), jnp.float32),
            dma,
            dma((n_blk, 2)), dma((n_blk, 2)), dma((n_own, 2)), dma((n_own, 2)),
            dma((n_blk,)), dma((n_blk,)), dma((n_own,)), dma((n_own,)),
        ],
        compiler_params=pltpu.CompilerParams(collective_id=0, has_side_effects=True),
    )(embeddings, clusters.reshape(1, n_rows), place.reshape(1, n_rows))
    return best.reshape(n_rows)


def solution(mesh):
    spread = ("parts", "blk", "owner", "sub")
    return jax.shard_map(
        body, mesh=mesh, in_specs=(P(spread, None), P(spread), P(spread)), out_specs=P(spread),
        check_vma=False)
```

```python
import functools
import math

import jax
import jax.numpy as jnp
from jax import lax
from jax.experimental import pallas as pl
from jax.experimental.pallas import tpu as pltpu
from jax.sharding import PartitionSpec as P

MESH = pl.DeviceIdType.MESH
LOWEST = -1.0


def each(start, stop, step):
    if stop - start <= 8:
        for index in range(start, stop):
            step(index)
    else:
        lax.fori_loop(start, stop, lambda index, _: (step(index), 0)[1], 0)


def pair_scores(mine, other):
    return lax.dot_general(
        mine, other, (((1,), (1,)), ((), ())), preferred_element_type=jnp.float32
    )


def div_rem(values, cap, n_own):
    return lax.rem(lax.div(values, jnp.int32(cap)), jnp.int32(n_own))


def kernel(
    n_blk, n_own, cap,
    emb_ref, clusters_ref, place_ref, out_ref,
    emb, clusters, place, rows, row_keys, cols, col_keys, best, down_keys,
    col_answer, col_back, row_answer, row_back,
    load_sem, col_send, col_recv, row_send, row_recv,
    col_back_send, col_back_recv, row_back_send, row_back_recv,
):
    n_rows, width = emb.shape
    z = lax.axis_index("blk")
    x = lax.axis_index("owner")
    sub = lax.axis_index("sub")

    def flows(a, b):
        low, apart = jnp.minimum(a, b), jnp.abs(a - b)
        up = (apart < n_blk - 1) & ((sub == 1) | (low == apart - 1))
        return ((a < b) & up) | ((a > b) & ~up)

    loads = [
        pltpu.make_async_copy(src, dst, load_sem.at[k])
        for k, (src, dst) in enumerate((
            (emb_ref, emb), (clusters_ref, clusters), (place_ref, place)))
    ]
    for load in loads:
        load.start()

    barrier = pltpu.get_barrier_semaphore()
    each(1, n_own, lambda e: pl.semaphore_signal(
        barrier, inc=1, device_id={"owner": lax.rem(x + e, n_own)}, device_id_type=MESH))

    def greet(a):
        @pl.when(flows(a, z))
        def _():
            pl.semaphore_signal(barrier, inc=1, device_id={"blk": a}, device_id_type=MESH)

    each(0, n_blk, greet)

    def col_copies(a, b):
        return [
            pltpu.make_async_remote_copy(
                src_ref=src, dst_ref=dst, send_sem=col_send.at[b, k], recv_sem=col_recv.at[a, k],
                device_id={"blk": b}, device_id_type=MESH)
            for k, (src, dst) in enumerate((
                (row_keys.at[0], col_keys.at[a]), (rows.at[pl.ds(0, n_rows)], cols.at[a])))
        ]

    def row_copies(e):
        target = {"owner": lax.rem(x + e, n_own)}
        return [
            pltpu.make_async_remote_copy(
                src_ref=src, dst_ref=dst, send_sem=row_send.at[e, k], recv_sem=row_recv.at[e, k],
                device_id=target, device_id_type=MESH)
            for k, (src, dst) in enumerate((
                (row_keys.at[0], row_keys.at[e]),
                (rows.at[pl.ds(0, n_rows)], rows.at[pl.ds(e * n_rows, n_rows)])))
        ]

    def col_return(a, b):
        return pltpu.make_async_remote_copy(
            src_ref=col_answer.at[a], dst_ref=col_back.at[b],
            send_sem=col_back_send.at[a], recv_sem=col_back_recv.at[b],
            device_id={"blk": a}, device_id_type=MESH)

    def row_return(e):
        return pltpu.make_async_remote_copy(
            src_ref=row_answer.at[e], dst_ref=row_back.at[e],
            send_sem=row_back_send.at[e], recv_sem=row_back_recv.at[e],
            device_id={"owner": lax.rem(x + n_own - e, n_own)}, device_id_type=MESH)

    def down(key):
        return jnp.transpose(jnp.broadcast_to(key, (n_rows, n_rows)))

    for load in loads:
        load.wait()
    group = div_rem(place[...], cap, n_own)
    my_key = group * 65536 + clusters[...]
    row_keys[0] = my_key
    values = emb[...].astype(jnp.float32)
    mean = jnp.mean(values * values, axis=1, keepdims=True)
    unit = values * (lax.rsqrt(mean + 1e-06) * (1.0 / math.sqrt(width)))
    rows[pl.ds(0, n_rows)] = unit.astype(jnp.bfloat16)

    targets = sum(flows(z, b).astype(jnp.int32) for b in range(n_blk))
    pl.semaphore_wait(barrier, targets + n_own - 1)

    def send_cols(b):
        @pl.when(flows(z, b))
        def _():
            for copy in col_copies(z, b):
                copy.start()

    each(0, n_blk, send_cols)

    def send_rows(e):
        for copy in row_copies(e):
            copy.start()

    each(1, n_own, send_rows)

    down_keys[pl.ds(0, n_rows)] = down(my_key)
    mine = rows[pl.ds(0, n_rows)]
    shape = (n_rows, n_rows)
    other = lax.broadcasted_iota(jnp.int32, shape, 0) != lax.broadcasted_iota(jnp.int32, shape, 1)
    best[pl.ds(0, n_rows)] = jnp.where(
        (down_keys[pl.ds(0, n_rows)] == my_key) & other, pair_scores(mine, mine), LOWEST)

    def meet_row(e):
        for copy in row_copies(e):
            copy.wait_recv()
        theirs = rows[pl.ds(e * n_rows, n_rows)]
        down_keys[pl.ds(e * n_rows, n_rows)] = down(row_keys[e])
        found = jnp.where(
            down_keys[pl.ds(0, n_rows)] == row_keys[e], pair_scores(mine, theirs), LOWEST)
        best[pl.ds(0, n_rows)] = jnp.maximum(best[pl.ds(0, n_rows)], found)
        best[pl.ds(e * n_rows, n_rows)] = jnp.full(shape, LOWEST, jnp.float32)

    each(1, n_own, meet_row)

    def meet_col(a):
        @pl.when(flows(a, z))
        def _():
            for copy in col_copies(a, z):
                copy.wait_recv()
            col_key = col_keys[a]
            scores = pair_scores(rows[...], cols[a])
            answer = None
            for e in range(n_own):
                here = pl.ds(e * n_rows, n_rows)
                found = jnp.where(
                    down_keys[here] == col_key, scores[e * n_rows:(e + 1) * n_rows], LOWEST)
                best[here] = jnp.maximum(best[here], found)
                top = jnp.max(found, axis=0, keepdims=True)
                answer = top if answer is None else jnp.maximum(answer, top)
            col_answer[a] = answer
            col_return(a, z).start()

    each(0, n_blk, meet_col)

    def answer_row(e):
        row_answer[e] = jnp.max(
            jnp.transpose(best[pl.ds(e * n_rows, n_rows)]), axis=0, keepdims=True)
        row_return(e).start()

    each(1, n_own, answer_row)

    out_ref[...] = jnp.max(jnp.transpose(best[pl.ds(0, n_rows)]), axis=0, keepdims=True)

    def take_col(b):
        @pl.when(flows(z, b))
        def _():
            for copy in col_copies(z, b):
                copy.wait_send()
            col_return(z, b).wait_recv()
            out_ref[...] = jnp.maximum(out_ref[...], col_back[b])

        @pl.when(flows(b, z))
        def _():
            col_return(b, z).wait_send()

    def take_row(e):
        for copy in row_copies(e):
            copy.wait_send()
        row_return(e).wait()
        out_ref[...] = jnp.maximum(out_ref[...], row_back[e])

    each(0, n_blk, take_col)
    each(1, n_own, take_row)


def body(embeddings, clusters, place):
    n_rows, width = embeddings.shape
    n_blk = lax.axis_size("blk")
    n_own = lax.axis_size("owner")
    cap = 2 * n_rows // (n_blk * n_own)
    vmem = pl.BlockSpec(memory_space=pltpu.VMEM)
    dma = pltpu.SemaphoreType.DMA
    best = pl.pallas_call(
        functools.partial(kernel, n_blk, n_own, cap),
        out_shape=pltpu.VMEM((1, n_rows), jnp.float32),
        in_specs=[pl.BlockSpec(memory_space=pltpu.HBM)] * 3,
        out_specs=vmem,
        scratch_shapes=[
            pltpu.VMEM((n_rows, width), jnp.bfloat16),
            pltpu.VMEM((1, n_rows), jnp.int32),
            pltpu.VMEM((1, n_rows), jnp.int32),
            pltpu.VMEM((n_own * n_rows, width), jnp.bfloat16),
            pltpu.VMEM((n_own, 1, n_rows), jnp.int32),
            pltpu.VMEM((n_blk, n_rows, width), jnp.bfloat16),
            pltpu.VMEM((n_blk, 1, n_rows), jnp.int32),
            pltpu.VMEM((n_own * n_rows, n_rows), jnp.float32),
            pltpu.VMEM((n_own * n_rows, n_rows), jnp.int32),
            pltpu.VMEM((n_blk, 1, n_rows), jnp.float32),
            pltpu.VMEM((n_blk, 1, n_rows), jnp.float32),
            pltpu.VMEM((n_own, 1, n_rows), jnp.float32),
            pltpu.VMEM((n_own, 1, n_rows), jnp.float32),
            dma((3,)),
            dma((n_blk, 2)), dma((n_blk, 2)), dma((n_own, 2)), dma((n_own, 2)),
            dma((n_blk,)), dma((n_blk,)), dma((n_own,)), dma((n_own,)),
        ],
        compiler_params=pltpu.CompilerParams(collective_id=0, has_side_effects=True),
    )(embeddings, clusters.reshape(1, n_rows), place.reshape(1, n_rows))
    return best.reshape(n_rows)


def solution(mesh):
    spread = ("parts", "blk", "owner", "sub")
    return jax.shard_map(
        body, mesh=mesh, in_specs=(P(spread, None), P(spread), P(spread)), out_specs=P(spread),
        check_vma=False)
```

```python
import functools
import math

import jax
import jax.numpy as jnp
from jax import lax
from jax.experimental import pallas as pl
from jax.experimental.pallas import tpu as pltpu
from jax.sharding import PartitionSpec as P

MESH = pl.DeviceIdType.MESH
LOWEST = -1.0


def each(start, stop, step):
    if stop - start <= 8:
        for index in range(start, stop):
            step(index)
    else:
        lax.fori_loop(start, stop, lambda index, _: (step(index), 0)[1], 0)


def pair_scores(mine, other):
    return lax.dot_general(
        mine, other, (((1,), (1,)), ((), ())), preferred_element_type=jnp.float32
    )


def div_rem(values, cap, n_own):
    return lax.rem(lax.div(values, jnp.int32(cap)), jnp.int32(n_own))


def kernel(
    n_blk, n_own, cap,
    emb_ref, clusters_ref, place_ref, out_ref,
    emb, rows, row_keys, cols, col_keys, answer,
    col_answer, col_back, row_back,
    load_sem, col_send, col_recv, row_send, row_recv,
    col_back_send, col_back_recv, row_back_send, row_back_recv,
):
    n_rows, width = emb.shape
    z = lax.axis_index("blk")
    x = lax.axis_index("owner")
    sub = lax.axis_index("sub")

    def flows(a, b):
        low, apart = jnp.minimum(a, b), jnp.abs(a - b)
        up = (apart < n_blk - 1) & ((sub == 0) | ((low == 1) & (apart == 1)))
        return ((a < b) & up) | ((a > b) & ~up)

    loads = [
        pltpu.make_async_copy(src, dst, load_sem.at[k])
        for k, (src, dst) in enumerate((
            (emb_ref, emb), (clusters_ref, row_keys.at[0, 0]), (place_ref, row_keys.at[0, 1])))
    ]
    for load in loads:
        load.start()

    barrier = pltpu.get_barrier_semaphore()
    each(1, n_own, lambda e: pl.semaphore_signal(
        barrier, inc=1, device_id={"owner": lax.rem(x + e, n_own)}, device_id_type=MESH))

    def greet(a):
        @pl.when(flows(a, z))
        def _():
            pl.semaphore_signal(barrier, inc=1, device_id={"blk": a}, device_id_type=MESH)

    each(0, n_blk, greet)

    def col_copy(a, b, k):
        src, dst = (
            (clusters_ref, col_keys.at[a, 0]), (place_ref, col_keys.at[a, 1]),
            (emb_ref, cols.at[a]))[k]
        return pltpu.make_async_remote_copy(
            src_ref=src, dst_ref=dst, send_sem=col_send.at[b, k], recv_sem=col_recv.at[a, k],
            device_id={"blk": b}, device_id_type=MESH)

    def row_copy(e, k):
        src, dst = (
            (clusters_ref, row_keys.at[e, 0]), (place_ref, row_keys.at[e, 1]),
            (emb_ref, rows.at[pl.ds(e * n_rows, n_rows)]))[k]
        return pltpu.make_async_remote_copy(
            src_ref=src, dst_ref=dst, send_sem=row_send.at[e, k], recv_sem=row_recv.at[e, k],
            device_id={"owner": lax.rem(x + e, n_own)}, device_id_type=MESH)

    def col_return(a, b):
        return pltpu.make_async_remote_copy(
            src_ref=col_answer.at[a], dst_ref=col_back.at[b],
            send_sem=col_back_send.at[a], recv_sem=col_back_recv.at[b],
            device_id={"blk": a}, device_id_type=MESH)

    def row_return(e):
        return pltpu.make_async_remote_copy(
            src_ref=answer.at[e], dst_ref=row_back.at[e],
            send_sem=row_back_send.at[e], recv_sem=row_back_recv.at[e],
            device_id={"owner": lax.rem(x + n_own - e, n_own)}, device_id_type=MESH)

    def down(key):
        return jnp.transpose(jnp.broadcast_to(key, (n_rows, n_rows)))

    def unit(block):
        values = block.astype(jnp.float32)
        mean = jnp.mean(values * values, axis=1, keepdims=True)
        scaled = values * (lax.rsqrt(mean + 1e-06) * (1.0 / math.sqrt(width)))
        return scaled.astype(jnp.bfloat16)

    def send_cols(b):
        @pl.when(flows(z, b))
        def _():
            for k in range(3):
                col_copy(z, b, k).start()

    def send_rows(e):
        for k in range(3):
            row_copy(e, k).start()

    def key_of(clusters, place):
        return div_rem(place, cap, n_own) * 65536 + clusters

    targets = sum(flows(z, b).astype(jnp.int32) for b in range(n_blk))
    pl.semaphore_wait(barrier, targets + n_own - 1)
    each(0, n_blk, send_cols)
    each(1, n_own, send_rows)

    for load in loads:
        load.wait()
    my_key = key_of(row_keys[0, 0], row_keys[0, 1])
    rows[pl.ds(0, n_rows)] = unit(emb[...])

    def top(found):
        return jnp.max(found, axis=0, keepdims=True)

    mine = rows[pl.ds(0, n_rows)]
    shape = (n_rows, n_rows)
    other = lax.broadcasted_iota(jnp.int32, shape, 0) != lax.broadcasted_iota(jnp.int32, shape, 1)
    answer[...] = jnp.full(answer.shape, LOWEST, jnp.float32)
    answer[0] = top(jnp.where((down(my_key) == my_key) & other, pair_scores(mine, mine), LOWEST))

    def meet_row(e):
        for k in range(3):
            row_copy(e, k).wait_recv()
        theirs = unit(rows[pl.ds(e * n_rows, n_rows)])
        rows[pl.ds(e * n_rows, n_rows)] = theirs
        found = jnp.where(down(key_of(row_keys[e, 0], row_keys[e, 1])) == my_key, pair_scores(theirs, mine), LOWEST)
        answer[0] = jnp.maximum(answer[0], top(found))

    each(1, n_own, meet_row)

    last = functools.reduce(
        jnp.maximum, [jnp.where(flows(a, z), a, -1) for a in range(n_blk)])

    def meet_col(a):
        @pl.when(flows(a, z))
        def _():
            for k in range(2):
                col_copy(a, z, k).wait_recv()
            col_down = down(key_of(col_keys[a, 0], col_keys[a, 1]))
            col_copy(a, z, 2).wait_recv()
            scores = pair_scores(unit(cols[a]), rows[...])
            best = None
            for e in range(n_own):
                found = jnp.where(
                    col_down == key_of(row_keys[e, 0], row_keys[e, 1]), scores[:, e * n_rows:(e + 1) * n_rows], LOWEST)
                answer[e] = jnp.maximum(answer[e], top(found))
                best = found if best is None else jnp.maximum(best, found)

            @pl.when(a == last)
            def _():
                each(1, n_own, lambda e: row_return(e).start())

            col_answer[a] = top(jnp.transpose(best))
            col_return(a, z).start()

    each(0, n_blk, meet_col)

    @pl.when(last < 0)
    def _():
        each(1, n_own, lambda e: row_return(e).start())

    out_ref[...] = answer[0]

    def take_col(b):
        @pl.when(flows(z, b))
        def _():
            for k in range(3):
                col_copy(z, b, k).wait_send()
            col_return(z, b).wait_recv()
            out_ref[...] = jnp.maximum(out_ref[...], col_back[b])

        @pl.when(flows(b, z))
        def _():
            col_return(b, z).wait_send()

    def take_row(e):
        for k in range(3):
            row_copy(e, k).wait_send()
        row_return(e).wait()
        out_ref[...] = jnp.maximum(out_ref[...], row_back[e])

    each(0, n_blk, take_col)
    each(1, n_own, take_row)


def body(embeddings, clusters, place):
    n_rows, width = embeddings.shape
    n_blk = lax.axis_size("blk")
    n_own = lax.axis_size("owner")
    cap = 2 * n_rows // (n_blk * n_own)
    vmem = pl.BlockSpec(memory_space=pltpu.VMEM)
    dma = pltpu.SemaphoreType.DMA
    best = pl.pallas_call(
        functools.partial(kernel, n_blk, n_own, cap),
        out_shape=pltpu.VMEM((1, n_rows), jnp.float32),
        in_specs=[pl.BlockSpec(memory_space=pltpu.HBM)] * 3,
        out_specs=vmem,
        scratch_shapes=[
            pltpu.VMEM((n_rows, width), jnp.bfloat16),
            pltpu.VMEM((n_own * n_rows, width), jnp.bfloat16),
            pltpu.VMEM((n_own, 2, 1, n_rows), jnp.int32),
            pltpu.VMEM((n_blk, n_rows, width), jnp.bfloat16),
            pltpu.VMEM((n_blk, 2, 1, n_rows), jnp.int32),
            pltpu.VMEM((n_own, 1, n_rows), jnp.float32),
            pltpu.VMEM((n_blk, 1, n_rows), jnp.float32),
            pltpu.VMEM((n_blk, 1, n_rows), jnp.float32),
            pltpu.VMEM((n_own, 1, n_rows), jnp.float32),
            dma((3,)),
            dma((n_blk, 3)), dma((n_blk, 3)), dma((n_own, 3)), dma((n_own, 3)),
            dma((n_blk,)), dma((n_blk,)), dma((n_own,)), dma((n_own,)),
        ],
        compiler_params=pltpu.CompilerParams(collective_id=0, has_side_effects=True),
    )(embeddings, clusters.reshape(1, n_rows), place.reshape(1, n_rows))
    return best.reshape(n_rows)


def solution(mesh):
    spread = ("parts", "blk", "owner", "sub")
    return jax.shard_map(
        body, mesh=mesh, in_specs=(P(spread, None), P(spread), P(spread)), out_specs=P(spread),
        check_vma=False)
```

```python
import functools
import math

import jax
import jax.numpy as jnp
from jax import lax
from jax.experimental import pallas as pl
from jax.experimental.pallas import tpu as pltpu
from jax.sharding import PartitionSpec as P

MESH = pl.DeviceIdType.MESH
LOWEST = -1.0


def each(start, stop, step):
    if stop - start <= 8:
        for index in range(start, stop):
            step(index)
    else:
        lax.fori_loop(start, stop, lambda index, _: (step(index), 0)[1], 0)


def pair_scores(mine, other):
    return lax.dot_general(
        mine, other, (((1,), (1,)), ((), ())), preferred_element_type=jnp.float32
    )


def div_rem(values, cap, n_own):
    return lax.rem(lax.div(values, jnp.int32(cap)), jnp.int32(n_own))


def kernel(
    n_blk, n_own, cap,
    emb_ref, clusters_ref, place_ref, out_ref,
    emb, rows, row_keys, cols, col_keys, answer,
    col_answer, col_back, row_back,
    load_sem, col_send, col_recv, row_send, row_recv,
    col_back_send, col_back_recv, row_back_send, row_back_recv,
):
    n_rows, width = emb.shape
    z = lax.axis_index("blk")
    x = lax.axis_index("owner")
    sub = lax.axis_index("sub")

    def flows(a, b):
        low, apart = jnp.minimum(a, b), jnp.abs(a - b)
        up = (apart < n_blk - 1) & jnp.where(
            sub == 0, (low == 0) | (apart == 2), (low == 1) & (apart == 1))
        return ((a < b) & up) | ((a > b) & ~up)

    loads = [
        pltpu.make_async_copy(src, dst, load_sem.at[k])
        for k, (src, dst) in enumerate((
            (emb_ref, emb), (clusters_ref, row_keys.at[0, 0]), (place_ref, row_keys.at[0, 1])))
    ]

    barrier = pltpu.get_barrier_semaphore()
    each(1, n_own, lambda e: pl.semaphore_signal(
        barrier, inc=1, device_id={"owner": lax.rem(x + e, n_own)}, device_id_type=MESH))

    def greet(a):
        @pl.when(flows(a, z))
        def _():
            pl.semaphore_signal(barrier, inc=1, device_id={"blk": a}, device_id_type=MESH)

    each(0, n_blk, greet)

    def col_copy(a, b, k):
        src, dst = (
            (clusters_ref, col_keys.at[a, 0]), (place_ref, col_keys.at[a, 1]),
            (emb_ref, cols.at[a]))[k]
        return pltpu.make_async_remote_copy(
            src_ref=src, dst_ref=dst, send_sem=col_send.at[b, k], recv_sem=col_recv.at[a, k],
            device_id={"blk": b}, device_id_type=MESH)

    def row_copy(e, k):
        src, dst = (
            (clusters_ref, row_keys.at[e, 0]), (place_ref, row_keys.at[e, 1]),
            (emb_ref, rows.at[pl.ds(e * n_rows, n_rows)]))[k]
        return pltpu.make_async_remote_copy(
            src_ref=src, dst_ref=dst, send_sem=row_send.at[e, k], recv_sem=row_recv.at[e, k],
            device_id={"owner": lax.rem(x + e, n_own)}, device_id_type=MESH)

    def col_return(a, b):
        return pltpu.make_async_remote_copy(
            src_ref=col_answer.at[a], dst_ref=col_back.at[b],
            send_sem=col_back_send.at[a], recv_sem=col_back_recv.at[b],
            device_id={"blk": a}, device_id_type=MESH)

    def row_return(e):
        return pltpu.make_async_remote_copy(
            src_ref=answer.at[e], dst_ref=row_back.at[e],
            send_sem=row_back_send.at[e], recv_sem=row_back_recv.at[e],
            device_id={"owner": lax.rem(x + n_own - e, n_own)}, device_id_type=MESH)

    def down(key):
        return jnp.transpose(jnp.broadcast_to(key, (n_rows, n_rows)))

    def unit(block):
        values = block.astype(jnp.float32)
        mean = jnp.mean(values * values, axis=1, keepdims=True)
        scaled = values * (lax.rsqrt(mean + 1e-06) * (1.0 / math.sqrt(width)))
        return scaled.astype(jnp.bfloat16)

    def send_cols(b):
        @pl.when(flows(z, b))
        def _():
            for k in range(3):
                col_copy(z, b, k).start()

    def send_rows(e):
        for k in range(3):
            row_copy(e, k).start()

    def key_of(clusters, place):
        return div_rem(place, cap, n_own) * 65536 + clusters

    targets = sum(flows(z, b).astype(jnp.int32) for b in range(n_blk))
    pl.semaphore_wait(barrier, targets + n_own - 1)
    each(0, n_blk, send_cols)
    each(1, n_own, send_rows)
    for load in loads:
        load.start()

    for load in loads:
        load.wait()
    my_key = key_of(row_keys[0, 0], row_keys[0, 1])
    rows[pl.ds(0, n_rows)] = unit(emb[...])

    def top(found):
        return jnp.max(found, axis=0, keepdims=True)

    mine = rows[pl.ds(0, n_rows)]
    shape = (n_rows, n_rows)
    other = lax.broadcasted_iota(jnp.int32, shape, 0) != lax.broadcasted_iota(jnp.int32, shape, 1)
    answer[...] = jnp.full(answer.shape, LOWEST, jnp.float32)
    answer[0] = top(jnp.where((down(my_key) == my_key) & other, pair_scores(mine, mine), LOWEST))

    def meet_row(e):
        for k in range(3):
            row_copy(e, k).wait_recv()
        theirs = unit(rows[pl.ds(e * n_rows, n_rows)])
        rows[pl.ds(e * n_rows, n_rows)] = theirs
        found = jnp.where(down(key_of(row_keys[e, 0], row_keys[e, 1])) == my_key, pair_scores(theirs, mine), LOWEST)
        answer[0] = jnp.maximum(answer[0], top(found))

    each(1, n_own, meet_row)

    last = functools.reduce(
        jnp.maximum, [jnp.where(flows(a, z), a, -1) for a in range(n_blk)])

    def meet_col(a):
        @pl.when(flows(a, z))
        def _():
            for k in range(2):
                col_copy(a, z, k).wait_recv()
            col_down = down(key_of(col_keys[a, 0], col_keys[a, 1]))
            col_copy(a, z, 2).wait_recv()
            scores = pair_scores(unit(cols[a]), rows[...])
            best = None
            for e in range(n_own):
                found = jnp.where(
                    col_down == key_of(row_keys[e, 0], row_keys[e, 1]), scores[:, e * n_rows:(e + 1) * n_rows], LOWEST)
                answer[e] = jnp.maximum(answer[e], top(found))
                best = found if best is None else jnp.maximum(best, found)

            @pl.when(a == last)
            def _():
                each(1, n_own, lambda e: row_return(e).start())

            col_answer[a] = top(jnp.transpose(best))
            col_return(a, z).start()

    each(0, n_blk, meet_col)

    @pl.when(last < 0)
    def _():
        each(1, n_own, lambda e: row_return(e).start())

    out_ref[...] = answer[0]

    def take_col(b):
        @pl.when(flows(z, b))
        def _():
            for k in range(3):
                col_copy(z, b, k).wait_send()
            col_return(z, b).wait_recv()
            out_ref[...] = jnp.maximum(out_ref[...], col_back[b])

        @pl.when(flows(b, z))
        def _():
            col_return(b, z).wait_send()

    def take_row(e):
        for k in range(3):
            row_copy(e, k).wait_send()
        row_return(e).wait()
        out_ref[...] = jnp.maximum(out_ref[...], row_back[e])

    each(0, n_blk, take_col)
    each(1, n_own, take_row)


def body(embeddings, clusters, place):
    n_rows, width = embeddings.shape
    n_blk = lax.axis_size("blk")
    n_own = lax.axis_size("owner")
    cap = 2 * n_rows // (n_blk * n_own)
    vmem = pl.BlockSpec(memory_space=pltpu.VMEM)
    dma = pltpu.SemaphoreType.DMA
    best = pl.pallas_call(
        functools.partial(kernel, n_blk, n_own, cap),
        out_shape=pltpu.VMEM((1, n_rows), jnp.float32),
        in_specs=[pl.BlockSpec(memory_space=pltpu.HBM)] * 3,
        out_specs=vmem,
        scratch_shapes=[
            pltpu.VMEM((n_rows, width), jnp.bfloat16),
            pltpu.VMEM((n_own * n_rows, width), jnp.bfloat16),
            pltpu.VMEM((n_own, 2, 1, n_rows), jnp.int32),
            pltpu.VMEM((n_blk, n_rows, width), jnp.bfloat16),
            pltpu.VMEM((n_blk, 2, 1, n_rows), jnp.int32),
            pltpu.VMEM((n_own, 1, n_rows), jnp.float32),
            pltpu.VMEM((n_blk, 1, n_rows), jnp.float32),
            pltpu.VMEM((n_blk, 1, n_rows), jnp.float32),
            pltpu.VMEM((n_own, 1, n_rows), jnp.float32),
            dma((3,)),
            dma((n_blk, 3)), dma((n_blk, 3)), dma((n_own, 3)), dma((n_own, 3)),
            dma((n_blk,)), dma((n_blk,)), dma((n_own,)), dma((n_own,)),
        ],
        compiler_params=pltpu.CompilerParams(collective_id=0, has_side_effects=True),
    )(embeddings, clusters.reshape(1, n_rows), place.reshape(1, n_rows))
    return best.reshape(n_rows)


def solution(mesh):
    spread = ("parts", "blk", "owner", "sub")
    return jax.shard_map(
        body, mesh=mesh, in_specs=(P(spread, None), P(spread), P(spread)), out_specs=P(spread),
        check_vma=False)
```
